32 devices in a mesh: parts: 1, dev: 32 (over z, y, x, core).
Axes of the slice: x: 2, y: 2, z: 4, core: 2. Of those that a mesh axis runs over, the one named last changes fastest.
Arguments:
- prompt_state: bfloat16 [32, 16, 128, 128], P(('parts', 'dev')), may hold values from -4 to 4
- conv_state: bfloat16 [32, 3, 4096], P(('parts', 'dev')), may hold values from -6 to 6
- slot_prompt: int32 [512], P(('parts', 'dev')), may hold values from 0 to 31, as said below
- mixed_input: bfloat16 [3, 512, 4096], P(None, ('parts', 'dev')), may hold values from -6 to 6
- output_gate: bfloat16 [3, 512, 2048], P(None, ('parts', 'dev')), may hold values from -6 to 6
- residual: bfloat16 [3, 512, 2048], P(None, ('parts', 'dev')), may hold values from -6 to 6
- beta_logit: float32 [3, 512, 16], P(None, ('parts', 'dev')), may hold values from -6 to 6
- decay_logit: float32 [3, 512, 16], P(None, ('parts', 'dev')), may hold values from -6 to 6
- decay_base: float32 [16], replicated, may hold values from -3 to 0.5
- decay_bias: float32 [16], replicated, may hold values from -2 to 0
- head_gain: float32 [128], replicated, may hold values from 0.1 to 1.9
- conv_weight: float32 [4, 4096], replicated, may hold values from -3 to 3
- out_weight: bfloat16 [2048, 2048], replicated, may hold values from -0.125 to 0.125
- post_gain: float32 [2048], replicated, may hold values from 0.1 to 1.9
- router: bfloat16 [2048, 32], replicated, may hold values from -0.375 to 0.375
- expert_gate: bfloat16 [32, 2048, 256], P('dev'), may hold values from -0.125 to 0.125
- expert_up: bfloat16 [32, 2048, 256], P('dev'), may hold values from -0.125 to 0.125
- expert_down: bfloat16 [32, 256, 2048], P('dev'), may hold values from -0.75 to 0.75
- route_ids: int32 [3, 512, 10], P(None, ('parts', 'dev')), may hold values from 0 to 31, all different within a row; in each aligned block of 16 rows (0 to 15, 16 to 31, ..., all dimensions but the last counted through in order) at most 10 rows name the same one
Outputs:
- layer_out: bfloat16 [3, 512, 2048], P(None, ('parts', 'dev'))
The draws below stay inside these ranges and needn't reach their ends.
Inputs may be any that keep to these rules, and one draw needn't show every extreme that they name: `slot_prompt`: prompt p is held by device p. The 16 slots of device d hold samples of prompts d - 1, d and d + 1 only; every device with both neighbours holds 1 to 9 samples of each neighbour's prompt; every prompt has 8 to 32 samples, some prompt exactly 8 and some exactly 32. `route_ids`: each row names 10 different experts. At one step the rows of one device name one expert at most 10 times, a bound that some block reaches at some step and device.
All inputs are finite; a program needn't handle non-finite values.
Results may differ from the reference program's by a relative error of at most 0.0052.
Values may be sent and summed in bfloat16 or wider, within the bound.
A program may use at most 128 MiB of HBM per device.

```python
import math
import jax
import jax.numpy as jnp
import numpy as np
from jax import lax

D = 2048
VH = 16
KH = 8
DK = 128
DV = 128
KERNEL = 4
EH = 256
TOP = 10
S_DEV = 16
STEPS = 3
CONV = 4096
PROMPTS = 32
SAMPLES = 512
EXPERTS = 32
CAP = 10


def shuffle_slots(sub_key):
    return jax.random.permutation(sub_key, S_DEV)


def draw_slot_prompt(key, part):
    base_key = jax.random.fold_in(key, 11)
    key_split = jax.random.split(base_key, 4)
    device_index = jnp.arange(PROMPTS, dtype=jnp.int32)
    left_take = jax.random.randint(key_split[0], (PROMPTS,), 1, 5).astype(jnp.int32)
    right_take = jax.random.randint(key_split[1], (PROMPTS,), 1, 5).astype(jnp.int32)
    special = jax.random.randint(key_split[2], (), 3, PROMPTS - 2).astype(jnp.int32)
    left_take = jnp.where(device_index == special, 1, left_take)
    right_take = jnp.where(device_index == special, 1, right_take)
    right_take = jnp.where(device_index == special - 1, 9, right_take)
    left_take = jnp.where(device_index == special - 1, 1, left_take)
    left_take = jnp.where(device_index == special + 1, 9, left_take)
    right_take = jnp.where(device_index == special + 1, 1, right_take)
    right_take = jnp.where(device_index == special - 2, 1, right_take)
    left_take = jnp.where(device_index == 0, 0, left_take)
    right_take = jnp.where(device_index == PROMPTS - 1, 0, right_take)
    slot_index = jnp.arange(S_DEV, dtype=jnp.int32)
    is_left = slot_index[None, :] < left_take[:, None]
    is_right = slot_index[None, :] >= (S_DEV - right_take)[:, None]
    owner_prompt = jnp.where(is_left, device_index[:, None] - 1, jnp.where(is_right, device_index[:, None] + 1, device_index[:, None]))
    slot_orders = jax.vmap(shuffle_slots)(jax.random.split(key_split[3], PROMPTS))
    owner_prompt = jnp.take_along_axis(owner_prompt, slot_orders, axis=1)
    return owner_prompt.reshape(PROMPTS * S_DEV).astype(jnp.int32)


def steps_of(stream_key, dims, cuts, least, high):
    def one(axis_at, shards_of):
        heights = jax.random.uniform(jax.random.fold_in(jax.random.fold_in(stream_key, 6), axis_at), (shards_of,), jnp.float32, least / len(cuts), high / len(cuts))
        return jnp.repeat(jnp.exp(heights), dims[axis_at] // shards_of).reshape((-1,) + (1,) * (len(dims) - axis_at - 1))

    factor_of = one(*cuts[0])
    for cut in cuts[1:]:
        factor_of = factor_of * one(*cut)
    return factor_of


def shared_out(own_key, own, number, rows, count, top, bound, slope):
    ranking = jax.random.permutation(own_key, count)
    crowded, usual = load_shares(count, rows * top, bound, slope, True), load_shares(count, rows * top, bound, slope, False)
    places = jnp.arange(count)

    def named(tallies, offset_by):
        used = int((tallies > 0).sum())
        fixed = max(1, used // 4)
        moved = fixed + (places - fixed + offset_by * (used - fixed)) % max(1, count - fixed)
        return jnp.zeros((count,), jnp.int32).at[ranking[jnp.where(places < fixed, places, moved)]].set(jnp.asarray(tallies, jnp.int32))

    tallies = jnp.where(number % 4 == 0, named(crowded, number // 4), named(usual, number - number // 4 - 1))
    mixed = jax.random.permutation(jax.random.fold_in(own, 3), count)
    source_of, sink = mixed[0:count // 2 * 2:2], mixed[1:count // 2 * 2:2]
    slack = jnp.minimum(tallies[source_of] - 1, bound - tallies[sink]) // 2
    slack = jnp.where((source_of == ranking[0]) | (sink == ranking[0]) | (tallies[sink] == 0), 0, jnp.maximum(slack, 0))
    moved = jax.random.randint(jax.random.fold_in(own, 4), (count // 2,), 0, 1 << 20) % (slack + 1)
    tallies = tallies.at[source_of].add(-moved).at[sink].add(moved)
    labels = jnp.searchsorted(jnp.cumsum(tallies), jnp.arange(rows * top), side="right").astype(jnp.int32)
    grid = labels.reshape(top, rows).T
    grid = grid[jax.random.permutation(jax.random.fold_in(own, 1), rows)]
    offset_by = jax.random.randint(jax.random.fold_in(own, 2), (rows, 1), 0, top)
    return jnp.take_along_axis(grid, (jnp.arange(top)[None, :] + offset_by) % top, axis=1)


def load_shares(count, total, most, skew, full):
    weights = [(1 << 20) // math.isqrt(standing ** skew) + 1 for standing in range(1, count + 1)]
    largest = most if full else min(most, max(-(-total // count), total * weights[0] // sum(weights)))
    least = 1 if total - largest >= count - 1 else 0
    given, rest = [largest] + [least] * (count - 1), total - largest - least * (count - 1)
    while rest > 0:
        free = [i for i in range(1, count) if given[i] < largest] or [i for i in range(1, count) if given[i] < most]
        pool, budget = sum([weights[i] for i in free]), rest
        for i in free:
            extra = min(most - given[i], max(1, budget * weights[i] // pool), rest)
            given[i] = given[i] + extra
            rest = rest - extra
    return np.array(given)


def noise(rng, dims, scale, most, pieces=(), kind=jnp.bfloat16):
    entries = scale * jax.random.normal(rng, dims, jnp.float32)
    if pieces:
        entries = entries * steps_of(rng, dims, pieces, -0.22, 0.18)
    return jnp.clip(entries, -most, most).astype(kind)


def setup_inputs(seed: int = 0, part: int = 0) -> dict:
    arg_keys = jax.random.split(jax.random.key(seed), 20)
    own_keys = jax.random.split(jax.random.fold_in(arg_keys[19], part), 20)
    prompt_state = noise(own_keys[0], (PROMPTS, VH, DK, DV), 0.25, 4.0, ((0, 32),))
    conv_state = noise(own_keys[1], (PROMPTS, KERNEL - 1, CONV), 1.0, 6.0, ((0, 32),))
    slot_prompt = draw_slot_prompt(jax.random.fold_in(jax.random.fold_in(arg_keys[19], part), 71), part)
    mixed_input = noise(own_keys[3], (STEPS, SAMPLES, CONV), 1.0, 6.0, ((1, 32),))
    output_gate = noise(own_keys[4], (STEPS, SAMPLES, VH * DV), 1.0, 6.0, ((1, 32),))
    residual = noise(own_keys[5], (STEPS, SAMPLES, D), 1.0, 6.0, ((1, 32),))
    beta_logit = noise(own_keys[6], (STEPS, SAMPLES, VH), 1.5, 6.0, ((1, 32),), jnp.float32)
    decay_logit = noise(own_keys[7], (STEPS, SAMPLES, VH), 1.0, 6.0, ((1, 32),), jnp.float32)
    decay_base = jnp.clip(jax.random.uniform(arg_keys[8], (VH,), jnp.float32, -3.0, 0.5), -3.0, 0.5)
    decay_bias = jnp.clip(jax.random.uniform(arg_keys[9], (VH,), jnp.float32, -2.0, 0.0), -2.0, 0.0)
    head_gain = jnp.clip(1.0 + 0.18 * jax.random.normal(arg_keys[10], (DV,), jnp.float32), 0.1, 1.9)
    conv_weight = noise(arg_keys[11], (KERNEL, CONV), KERNEL ** -0.5, 3.0, (), jnp.float32)
    out_weight = noise(arg_keys[12], (VH * DV, D), (VH * DV) ** -0.5, 0.125)
    post_gain = jnp.clip(1.0 + 0.18 * jax.random.normal(arg_keys[13], (D,), jnp.float32), 0.1, 1.9)
    router = noise(arg_keys[14], (D, EXPERTS), (D // 8) ** -0.5, 0.375)
    expert_gate = noise(arg_keys[15], (EXPERTS, D, EH), D ** -0.5, 0.125, ((0, 32),))
    expert_up = noise(arg_keys[16], (EXPERTS, D, EH), D ** -0.5, 0.125, ((0, 32),))
    expert_down = noise(arg_keys[17], (EXPERTS, EH, D), (EH // 4) ** -0.5, 0.75, ((0, 32),))
    route_ids_keys = jax.random.split(jax.random.fold_in(own_keys[18], 1), STEPS * SAMPLES // S_DEV)
    route_ids_turns = jax.random.permutation(jax.random.fold_in(own_keys[18], 3), STEPS * SAMPLES // S_DEV)
    route_ids = jax.vmap(lambda own, number: shared_out(jax.random.fold_in(own_keys[18], 2), own, number, S_DEV, EXPERTS, TOP, CAP, 2))(route_ids_keys, route_ids_turns).reshape((STEPS, SAMPLES, TOP))
    return {"prompt_state": prompt_state, "conv_state": conv_state, "slot_prompt": slot_prompt, "mixed_input": mixed_input, "output_gate": output_gate, "residual": residual, "beta_logit": beta_logit, "decay_logit": decay_logit, "decay_base": decay_base, "decay_bias": decay_bias, "head_gain": head_gain, "conv_weight": conv_weight, "out_weight": out_weight, "post_gain": post_gain, "router": router, "expert_gate": expert_gate, "expert_up": expert_up, "expert_down": expert_down, "route_ids": route_ids}


epsilon = 1e-06

def conv_advance(conv_rows, incoming, conv_weight):
    window = jnp.concatenate([conv_rows, incoming[:, None, :]], axis=1)
    activated = jax.nn.silu(lax.optimization_barrier(jnp.sum(window * conv_weight[None], axis=1)))
    return (window[:, 1:], activated)

def delta_advance(memory, activated, output_gate, beta_logit, decay_logit, decay_base, decay_bias, head_gain):
    batch_size = activated.shape[0]
    key_width = KH * DK
    query_vec = activated[:, :key_width].reshape(batch_size, KH, DK)
    key_vec = activated[:, key_width:2 * key_width].reshape(batch_size, KH, DK)
    value_vec = activated[:, 2 * key_width:].reshape(batch_size, VH, DV)
    query_vec = query_vec * lax.rsqrt(lax.optimization_barrier(jnp.sum(query_vec * query_vec, axis=-1, keepdims=True)) + epsilon) * (1.0 / math.sqrt(DK))
    key_vec = key_vec * lax.rsqrt(lax.optimization_barrier(jnp.sum(key_vec * key_vec, axis=-1, keepdims=True)) + epsilon)
    query_vec = jnp.repeat(query_vec, VH // KH, axis=1)
    key_vec = jnp.repeat(key_vec, VH // KH, axis=1)
    strength = jax.nn.sigmoid(beta_logit)
    retain = jnp.exp(-jnp.exp(decay_base) * jax.nn.softplus(decay_logit + decay_bias))
    memory = memory * retain[:, :, None, None]
    recalled = lax.optimization_barrier(jnp.sum(memory * key_vec[..., None], axis=2))
    update = strength[..., None] * (value_vec - recalled)
    memory = memory + key_vec[..., None] * update[:, :, None, :]
    readout = lax.optimization_barrier(jnp.sum(memory * query_vec[..., None], axis=2))
    readout = readout * lax.rsqrt(lax.optimization_barrier(jnp.mean(readout * readout, axis=-1, keepdims=True)) + epsilon) * head_gain
    readout = readout * jax.nn.silu(output_gate.astype(jnp.float32).reshape(batch_size, VH, DV))
    return (memory, readout.reshape(batch_size, VH * DV).astype(jnp.bfloat16))

def residual_norm(carried, post_gain):
    scaled = carried * lax.rsqrt(lax.optimization_barrier(jnp.mean(carried * carried, axis=-1, keepdims=True)) + epsilon) * post_gain
    return scaled.astype(jnp.bfloat16)

def reference(prompt_state, conv_state, slot_prompt, mixed_input, output_gate, residual, beta_logit, decay_logit, decay_base, decay_bias, head_gain, conv_weight, out_weight, post_gain, router, expert_gate, expert_up, expert_down, route_ids):

    def decode_block(block_index):
        block_start = (block_index * S_DEV).astype(jnp.int32)
        prompts = lax.dynamic_slice_in_dim(slot_prompt, block_start, S_DEV)
        memory = prompt_state[prompts].astype(jnp.float32)
        conv_rows = conv_state[prompts].astype(jnp.float32)
        carried_list = []
        normed_list = []
        for step_index in range(STEPS):
            incoming = lax.dynamic_slice_in_dim(mixed_input[step_index], block_start, S_DEV).astype(jnp.float32)
            gate_rows = lax.dynamic_slice_in_dim(output_gate[step_index], block_start, S_DEV)
            beta_rows = lax.dynamic_slice_in_dim(beta_logit[step_index], block_start, S_DEV)
            decay_rows = lax.dynamic_slice_in_dim(decay_logit[step_index], block_start, S_DEV)
            resid_rows = lax.dynamic_slice_in_dim(residual[step_index], block_start, S_DEV)
            conv_rows, activated = conv_advance(conv_rows, incoming, conv_weight)
            memory, gated_out = delta_advance(memory, activated, gate_rows, beta_rows, decay_rows, decay_base, decay_bias, head_gain)
            carried = resid_rows.astype(jnp.float32) + jnp.dot(gated_out, out_weight, preferred_element_type=jnp.float32)
            carried_list.append(carried)
            normed_list.append(residual_norm(carried, post_gain))
        return (jnp.stack(carried_list), jnp.stack(normed_list))
    carried, normed = lax.map(decode_block, jnp.arange(SAMPLES // S_DEV, dtype=jnp.int32))
    carried = jnp.transpose(carried, (1, 0, 2, 3)).reshape(STEPS * SAMPLES, D)
    tokens = jnp.transpose(normed, (1, 0, 2, 3)).reshape(STEPS * SAMPLES, D)
    flat_ids = route_ids.reshape(STEPS * SAMPLES, TOP)
    logits = jnp.dot(tokens, router, preferred_element_type=jnp.float32)
    chosen = jnp.take_along_axis(logits, flat_ids, axis=1)
    gate_value = jax.nn.sigmoid(chosen)
    weights = gate_value / lax.optimization_barrier(jnp.sum(gate_value, axis=1, keepdims=True))
    row_limit = STEPS * (SAMPLES // S_DEV) * CAP

    def one_expert(accumulated, expert_index):
        route_hit = flat_ids == expert_index
        token_weight = lax.optimization_barrier(jnp.sum(jnp.where(route_hit, weights, 0.0), axis=1))
        is_routed = jnp.any(route_hit, axis=1)
        where_rows = jnp.nonzero(is_routed, size=row_limit, fill_value=0)[0]
        is_valid = (jnp.arange(row_limit) < jnp.sum(is_routed)).astype(jnp.float32)
        token_rows = tokens[where_rows]
        hidden = jax.nn.silu(jnp.dot(token_rows, expert_gate[expert_index], preferred_element_type=jnp.float32))
        hidden = (hidden * jnp.dot(token_rows, expert_up[expert_index], preferred_element_type=jnp.float32)).astype(jnp.bfloat16)
        out_rows = jnp.dot(hidden, expert_down[expert_index], preferred_element_type=jnp.float32).astype(jnp.bfloat16).astype(jnp.float32)
        scaled = out_rows * (token_weight[where_rows] * is_valid)[:, None]
        return (accumulated.at[where_rows].add(scaled), None)
    accumulated, unused = lax.scan(one_expert, jnp.zeros((STEPS * SAMPLES, D), jnp.float32), jnp.arange(EXPERTS, dtype=jnp.int32))
    return (carried + accumulated).astype(jnp.bfloat16).reshape(STEPS, SAMPLES, D)
```

```python
import math

import jax
import jax.numpy as jnp
from jax import lax
from jax.experimental import pallas as pl
from jax.experimental.pallas import tpu as pltpu
from jax.sharding import PartitionSpec as P

epsilon = 1e-06


def halves(x):
    high = lax.reduce_precision(x, 8, 7)
    return high, x - high


def delta_kernel(
    offset_ref, low_state, own_state, high_state, low_conv, own_conv, high_conv,
    mixed_ref, gate_ref, strength_ref, retain_ref, gain_ref, weight_ref, out_ref,
):
    steps, slots, _ = mixed_ref.shape
    heads, key_size, value_size = own_state.shape[1:]
    taps, channels = weight_ref.shape
    key_heads = (channels - heads * value_size) // (2 * key_size)
    share = heads // key_heads
    key_width = key_heads * key_size
    offset = offset_ref[...]
    is_low, is_high = offset == 0, offset == 2
    all_low = jnp.concatenate([is_low] * (4 * steps), axis=0)
    all_high = jnp.concatenate([is_high] * (4 * steps), axis=0)
    gain = gain_ref[...]

    def convolved(start, width):
        columns = slice(start, start + width)
        rows = []
        for j in range(taps - 1):
            own, low, high = (
                r[0, j : j + 1, columns].astype(jnp.float32) for r in (own_conv, low_conv, high_conv)
            )
            rows.append(jnp.where(is_low, low, jnp.where(is_high, high, own)))
        for t in range(steps):
            rows.append(mixed_ref[t, :, columns].astype(jnp.float32))
        results = []
        for t in range(steps):
            total = rows[t] * weight_ref[0:1, columns]
            for j in range(1, taps):
                total = total + rows[t + j] * weight_ref[j : j + 1, columns]
            results.append(total * jax.nn.sigmoid(total))
        return results

    def summed(x):
        return jnp.sum(x, axis=-1, keepdims=True)

    for group in range(key_heads):
        query = [
            x * (lax.rsqrt(summed(x * x) + epsilon) * (1.0 / math.sqrt(key_size)))
            for x in convolved(group * key_size, key_size)
        ]
        key = [
            x * lax.rsqrt(summed(x * x) + epsilon)
            for x in convolved(key_width + group * key_size, key_size)
        ]
        parts = []
        for x in query + key:
            high = x.astype(jnp.bfloat16)
            parts += [high, (x - high.astype(jnp.float32)).astype(jnp.bfloat16)]
        stacked = jnp.concatenate(parts, axis=0)
        query_key = [[summed(query[t] * key[j]) for j in range(t + 1)] for t in range(steps)]
        key_key = [[summed(key[t] * key[j]) for j in range(t)] for t in range(steps)]
        for head in range(group * share, (group + 1) * share):
            low, own, high = (
                jnp.dot(stacked, r[0, head], preferred_element_type=jnp.float32)
                for r in (low_state, own_state, high_state)
            )
            product = jnp.where(all_low, low, jnp.where(all_high, high, own))
            read = [
                product[2 * i * slots : (2 * i + 1) * slots]
                + product[(2 * i + 1) * slots : (2 * i + 2) * slots]
                for i in range(2 * steps)
            ]
            value = convolved(2 * key_width + head * value_size, value_size)
            columns = slice(head * value_size, (head + 1) * value_size)
            updates = []
            for t in range(steps):
                recalled, readout = read[steps + t], read[t]
                for j in range(t + 1):
                    retain = retain_ref[j, :, head : head + 1]
                    recalled, readout = recalled * retain, readout * retain
                    if j < t:
                        recalled = recalled + key_key[t][j] * updates[j]
                        readout = readout + query_key[t][j] * updates[j]
                update = strength_ref[t, :, head : head + 1] * (value[t] - recalled)
                updates.append(update)
                readout = readout + query_key[t][t] * update
                readout = (
                    readout
                    * lax.rsqrt(summed(readout * readout) * (1.0 / value_size) + epsilon)
                    * gain
                )
                opened = gate_ref[t, :, columns].astype(jnp.float32)
                readout = readout * (opened * jax.nn.sigmoid(opened))
                out_ref[t * slots : (t + 1) * slots, columns] = readout.astype(out_ref.dtype)


def body(
    prompt_state, conv_state, slot_prompt, mixed_input, output_gate, residual, beta_logit,
    decay_logit, decay_base, decay_bias, head_gain, conv_weight, out_weight, post_gain, router,
    expert_gate, expert_up, expert_down, route_ids,
):
    steps, slots, width = residual.shape
    count = lax.axis_size("dev")
    me = lax.axis_index("dev")
    rows = steps * slots
    forward = [(i, i + 1) for i in range(count - 1)]
    backward = [(i + 1, i) for i in range(count - 1)]
    low_conv = lax.ppermute(conv_state, "dev", forward)
    high_conv = lax.ppermute(conv_state, "dev", backward)
    low_state = lax.ppermute(prompt_state, "dev", forward)
    high_state = lax.ppermute(prompt_state, "dev", backward)
    offset = (slot_prompt - (me - 1)).reshape(slots, 1)
    strength = jax.nn.sigmoid(beta_logit)
    retain = jnp.exp(-jnp.exp(decay_base) * jax.nn.softplus(decay_logit + decay_bias))
    heads, value_size = prompt_state.shape[1], prompt_state.shape[3]
    gated = pl.pallas_call(
        delta_kernel,
        out_shape=jax.ShapeDtypeStruct((rows, heads * value_size), jnp.bfloat16),
        in_specs=[pl.BlockSpec(memory_space=pltpu.VMEM)] * 13,
        out_specs=pl.BlockSpec(memory_space=pltpu.VMEM),
        compiler_params=pltpu.CompilerParams(vmem_limit_bytes=24 * 1024 * 1024),
    )(
        offset, low_state, prompt_state, high_state, low_conv, conv_state, high_conv,
        mixed_input, output_gate, strength, retain, head_gain.reshape(1, -1), conv_weight,
    )
    carried = residual.reshape(rows, width).astype(jnp.float32) + jnp.dot(
        gated, out_weight, preferred_element_type=jnp.float32
    )
    normed = (
        carried
        * lax.rsqrt(jnp.mean(carried * carried, axis=-1, keepdims=True) + epsilon)
        * post_gain
    ).astype(jnp.bfloat16)
    experts = router.shape[1]
    logits = jnp.dot(normed, router, preferred_element_type=jnp.float32)
    chosen = jnp.any(
        route_ids.reshape(rows, -1, 1) == jnp.arange(experts, dtype=jnp.int32), axis=1
    )
    weights = jnp.where(chosen, jax.nn.sigmoid(logits), 0.0)
    weights = weights / jnp.sum(weights, axis=1, keepdims=True)
    high, low = halves(weights)
    extra = -(-2 * experts // 128) * 128
    tail = jnp.concatenate(
        [high, low, jnp.zeros((rows, extra - 2 * experts), jnp.float32)], axis=1
    ).astype(jnp.bfloat16)
    gathered = lax.all_gather(jnp.concatenate([normed, tail], axis=1), "dev", axis=0, tiled=True)
    tokens = gathered[:, :width]
    column = jnp.arange(extra, dtype=jnp.int32)
    mine = (column == me) | (column == me + experts)
    weight = jnp.sum(
        jnp.where(mine, gathered[:, width:].astype(jnp.float32), 0.0), axis=1, keepdims=True
    )
    hidden = jax.nn.silu(jnp.dot(tokens, expert_gate[0], preferred_element_type=jnp.float32))
    hidden = hidden * jnp.dot(tokens, expert_up[0], preferred_element_type=jnp.float32)
    result = jnp.dot(
        hidden.astype(jnp.bfloat16), expert_down[0], preferred_element_type=jnp.float32
    )
    result = (result * weight).astype(jnp.bfloat16)
    mixture = lax.psum_scatter(result, "dev", scatter_dimension=0, tiled=True)
    layer_out = (carried + mixture.astype(jnp.float32)).astype(jnp.bfloat16)
    return layer_out.reshape(steps, slots, width)


def solution(mesh):
    split = P(None, ("parts", "dev"), None)
    in_specs = (
        P(("parts", "dev"), None, None, None),
        P(("parts", "dev"), None, None),
        P(("parts", "dev")),
        split, split, split, split, split,
        P(), P(), P(), P(), P(), P(), P(),
        P("dev", None, None),
        P("dev", None, None),
        P("dev", None, None),
        split,
    )
    return jax.shard_map(body, mesh=mesh, in_specs=in_specs, out_specs=split, check_vma=False)
```

```python
import functools
import math

import jax
import jax.numpy as jnp
from jax import lax
from jax.experimental import pallas as pl
from jax.experimental.pallas import tpu as pltpu
from jax.sharding import PartitionSpec as P

epsilon = 1e-06


def halves(x):
    high = lax.reduce_precision(x, 8, 7)
    return high, x - high


def delta_kernel(
    offset_ref, low_state, own_state, high_state, low_conv, own_conv, high_conv,
    mixed_ref, gate_ref, strength_ref, retain_ref, gain_ref, weight_ref, out_ref,
):
    steps, slots, _ = mixed_ref.shape
    heads, key_size, value_size = own_state.shape[1:]
    taps, channels = weight_ref.shape
    key_heads = (channels - heads * value_size) // (2 * key_size)
    share = heads // key_heads
    key_width = key_heads * key_size
    offset = offset_ref[...]
    is_low, is_high = offset == 0, offset == 2
    all_low = jnp.concatenate([is_low] * (4 * steps), axis=0)
    all_high = jnp.concatenate([is_high] * (4 * steps), axis=0)
    gain = gain_ref[...]

    def convolved(start, width):
        columns = slice(start, start + width)
        rows = []
        for j in range(taps - 1):
            own, low, high = (
                r[0, j : j + 1, columns].astype(jnp.float32) for r in (own_conv, low_conv, high_conv)
            )
            rows.append(jnp.where(is_low, low, jnp.where(is_high, high, own)))
        for t in range(steps):
            rows.append(mixed_ref[t, :, columns].astype(jnp.float32))
        results = []
        for t in range(steps):
            total = rows[t] * weight_ref[0:1, columns]
            for j in range(1, taps):
                total = total + rows[t + j] * weight_ref[j : j + 1, columns]
            results.append(total * jax.nn.sigmoid(total))
        return results

    def summed(x):
        return jnp.sum(x, axis=-1, keepdims=True)

    for group in range(key_heads):
        query = [
            x * (lax.rsqrt(summed(x * x) + epsilon) * (1.0 / math.sqrt(key_size)))
            for x in convolved(group * key_size, key_size)
        ]
        key = [
            x * lax.rsqrt(summed(x * x) + epsilon)
            for x in convolved(key_width + group * key_size, key_size)
        ]
        parts = []
        for x in query + key:
            high = x.astype(jnp.bfloat16)
            parts += [high, (x - high.astype(jnp.float32)).astype(jnp.bfloat16)]
        stacked = jnp.concatenate(parts, axis=0)
        query_key = [[summed(query[t] * key[j]) for j in range(t + 1)] for t in range(steps)]
        key_key = [[summed(key[t] * key[j]) for j in range(t)] for t in range(steps)]
        for head in range(group * share, (group + 1) * share):
            low, own, high = (
                jnp.dot(stacked, r[0, head], preferred_element_type=jnp.float32)
                for r in (low_state, own_state, high_state)
            )
            product = jnp.where(all_low, low, jnp.where(all_high, high, own))
            read = [
                product[2 * i * slots : (2 * i + 1) * slots]
                + product[(2 * i + 1) * slots : (2 * i + 2) * slots]
                for i in range(2 * steps)
            ]
            value = convolved(2 * key_width + head * value_size, value_size)
            columns = slice(head * value_size, (head + 1) * value_size)
            updates = []
            for t in range(steps):
                recalled, readout = read[steps + t], read[t]
                for j in range(t + 1):
                    retain = retain_ref[j, :, head : head + 1]
                    recalled, readout = recalled * retain, readout * retain
                    if j < t:
                        recalled = recalled + key_key[t][j] * updates[j]
                        readout = readout + query_key[t][j] * updates[j]
                update = strength_ref[t, :, head : head + 1] * (value[t] - recalled)
                updates.append(update)
                readout = readout + query_key[t][t] * update
                readout = (
                    readout
                    * lax.rsqrt(summed(readout * readout) * (1.0 / value_size) + epsilon)
                    * gain
                )
                opened = gate_ref[t, :, columns].astype(jnp.float32)
                readout = readout * (opened * jax.nn.sigmoid(opened))
                out_ref[t * slots : (t + 1) * slots, columns] = readout.astype(out_ref.dtype)


GATHER_ORDERS = (("z", "x", "y"), ("z", "y", "x"), ("y", "z", "x"))


class Place:
    def __init__(self, count):
        self.depth = count // 8
        self.me = lax.axis_index("dev")
        self.core = self.me % 2
        self.own = {"x": (self.me // 2) % 2, "y": (self.me // 4) % 2, "z": self.me // 8}
        self.sibling = self.me + 1 - 2 * self.core

    def partners(self, axis):
        if axis == "x":
            return [(self.me + 2 - 4 * self.own["x"], 1 - self.own["x"], 1 - self.own["x"])]
        if axis == "y":
            return [(self.me + 4 - 8 * self.own["y"], 1 - self.own["y"], 1 - self.own["y"])]
        found = []
        for k in range(1, self.depth):
            target = (self.own["z"] + k) % self.depth
            source = (self.own["z"] + self.depth - k) % self.depth
            found.append((target * 8 + self.me % 8, target, source))
        return found

    def meet(self):
        barrier = pltpu.get_barrier_semaphore()
        others = [self.sibling] + [p[0] for a in ("x", "y", "z") for p in self.partners(a)]
        for other in others:
            pl.semaphore_signal(
                barrier, inc=1, device_id={"dev": other}, device_id_type=pl.DeviceIdType.MESH
            )
        pl.semaphore_wait(barrier, len(others))


LANES = {"x": 0, "y": 1, "core": 2, "z": 3}


def remote(source, target, send, receive, device):
    return pltpu.make_async_remote_copy(
        src_ref=source, dst_ref=target, send_sem=send, recv_sem=receive,
        device_id={"dev": device}, device_id_type=pl.DeviceIdType.MESH,
    )


def gather_kernel(count, in_ref, out_ref, local_sem, send_sem, recv_sem):
    steps = in_ref.shape[0]
    place = Place(count)
    own = place.own
    local = []
    for t in range(steps):
        copy = pltpu.make_async_copy(
            in_ref.at[t], out_ref.at[t, own["z"], own["y"], own["x"], place.core], local_sem.at[t]
        )
        copy.start()
        local.append(copy)
    place.meet()
    sent = []
    arriving = [[] for _ in range(steps)]
    for stage in range(3):
        for t in range(steps):
            order = GATHER_ORDERS[t % 3]
            if stage == 0:
                local[t].wait()
            for copy in arriving[t]:
                copy.wait_recv()
            arriving[t] = []
            axis = order[stage]
            done = order[:stage]

            def region(position):
                at = [slice(None) if a in done else own[a] for a in ("z", "y", "x")]
                at[("z", "y", "x").index(axis)] = position
                return out_ref.at[t, at[0], at[1], at[2], place.core]

            for k, (device, _, source) in enumerate(place.partners(axis)):
                lane = LANES[axis] + k
                copy = remote(
                    region(own[axis]), region(own[axis]), send_sem.at[t, lane],
                    recv_sem.at[t, lane], device,
                )
                copy.start()
                sent.append(copy)
                arriving[t].append(
                    remote(
                        region(source), region(source), send_sem.at[t, lane],
                        recv_sem.at[t, lane], device,
                    )
                )
    last = []
    for t in range(steps):
        for copy in arriving[t]:
            copy.wait_recv()
        plane = out_ref.at[t, :, :, :, place.core]
        other = out_ref.at[t, :, :, :, 1 - place.core]
        sems = (send_sem.at[t, LANES["core"]], recv_sem.at[t, LANES["core"]], place.sibling)
        copy = remote(plane, plane, *sems)
        copy.start()
        sent.append(copy)
        last.append(remote(other, other, *sems))
    for copy in last:
        copy.wait_recv()
    for copy in sent:
        copy.wait_send()


def scatter_kernel(
    count, in_ref, out_ref, total, from_core, from_x, from_y, from_z, send_sem, recv_sem
):
    steps = in_ref.shape[0]
    place = Place(count)
    own = place.own
    place.meet()
    sent = []
    arriving = []
    for t in range(steps):
        copy = remote(
            in_ref.at[t, :, :, :, 1 - place.core], from_core.at[t],
            send_sem.at[t, LANES["core"]], recv_sem.at[t, LANES["core"]], place.sibling,
        )
        copy.start()
        sent.append(copy)
        arriving.append([copy])
    landed = [None] * steps
    for stage in range(4):
        for t in range(steps):
            order = GATHER_ORDERS[t % 3][::-1]
            for copy in arriving[t]:
                copy.wait_recv()
            arriving[t] = []
            done = order[:stage]
            at = [own[a] if a in done else slice(None) for a in ("z", "y", "x")]
            if stage == 0:
                value = in_ref[t, :, :, :, place.core].astype(jnp.float32)
                value = value + from_core[t].astype(jnp.float32)
            else:
                value = total[t, at[0], at[1], at[2]].astype(jnp.float32)
                for ref, index in landed[t]:
                    value = value + ref[index].astype(jnp.float32)
            if stage == 3:
                out_ref[t] = value
                continue
            total[t, at[0], at[1], at[2]] = value.astype(total.dtype)
            axis = order[stage]
            landed[t] = []
            for k, (device, target, _) in enumerate(place.partners(axis)):
                spot = dict(zip(("z", "y", "x"), at))
                source = dict(spot)
                source[axis] = target
                if axis == "x":
                    buffer, index = from_x, (t, spot["z"], spot["y"])
                elif axis == "y":
                    buffer, index = from_y, (t, spot["z"], spot["x"])
                else:
                    buffer, index = from_z, (t, k, spot["y"], spot["x"])
                lane = LANES[axis] + k
                copy = remote(
                    total.at[t, source["z"], source["y"], source["x"]], buffer.at[index],
                    send_sem.at[t, lane], recv_sem.at[t, lane], device,
                )
                copy.start()
                sent.append(copy)
                arriving[t].append(copy)
                landed[t].append((buffer, index))
    for copy in sent:
        copy.wait_send()


def gathered_rows(rows, count):
    steps, slots, width = rows.shape
    depth = count // 8
    sems = pltpu.SemaphoreType.DMA((steps, 2 + depth))
    return pl.pallas_call(
        functools.partial(gather_kernel, count),
        out_shape=jax.ShapeDtypeStruct((steps, depth, 2, 2, 2, slots, width), rows.dtype),
        in_specs=[pl.BlockSpec(memory_space=pl.ANY)],
        out_specs=pl.BlockSpec(memory_space=pl.ANY),
        scratch_shapes=[pltpu.SemaphoreType.DMA((steps,)), sems, sems],
        compiler_params=pltpu.CompilerParams(collective_id=0, has_side_effects=True),
    )(rows)


def scattered_sum(parts, count):
    steps, depth, _, _, _, slots, width = parts.shape
    sems = pltpu.SemaphoreType.DMA((steps, 2 + depth))
    return pl.pallas_call(
        functools.partial(scatter_kernel, count),
        out_shape=jax.ShapeDtypeStruct((steps, slots, width), jnp.float32),
        in_specs=[pl.BlockSpec(memory_space=pltpu.VMEM)],
        out_specs=pl.BlockSpec(memory_space=pltpu.VMEM),
        scratch_shapes=[
            pltpu.VMEM((steps, depth, 2, 2, slots, width), parts.dtype),
            pltpu.VMEM((steps, depth, 2, 2, slots, width), parts.dtype),
            pltpu.VMEM((steps, depth, 2, slots, width), parts.dtype),
            pltpu.VMEM((steps, depth, 2, slots, width), parts.dtype),
            pltpu.VMEM((steps, depth - 1, 2, 2, slots, width), parts.dtype),
            sems,
            sems,
        ],
        compiler_params=pltpu.CompilerParams(
            collective_id=1, has_side_effects=True, vmem_limit_bytes=56 * 1024 * 1024
        ),
    )(parts)


def body(
    prompt_state, conv_state, slot_prompt, mixed_input, output_gate, residual, beta_logit,
    decay_logit, decay_base, decay_bias, head_gain, conv_weight, out_weight, post_gain, router,
    expert_gate, expert_up, expert_down, route_ids,
):
    steps, slots, width = residual.shape
    count = lax.axis_size("dev")
    me = lax.axis_index("dev")
    rows = steps * slots
    forward = [(i, i + 1) for i in range(count - 1)]
    backward = [(i + 1, i) for i in range(count - 1)]
    low_conv = lax.ppermute(conv_state, "dev", forward)
    high_conv = lax.ppermute(conv_state, "dev", backward)
    low_state = lax.ppermute(prompt_state, "dev", forward)
    high_state = lax.ppermute(prompt_state, "dev", backward)
    offset = (slot_prompt - (me - 1)).reshape(slots, 1)
    strength = jax.nn.sigmoid(beta_logit)
    retain = jnp.exp(-jnp.exp(decay_base) * jax.nn.softplus(decay_logit + decay_bias))
    heads, value_size = prompt_state.shape[1], prompt_state.shape[3]
    gated = pl.pallas_call(
        delta_kernel,
        out_shape=jax.ShapeDtypeStruct((rows, heads * value_size), jnp.bfloat16),
        in_specs=[pl.BlockSpec(memory_space=pltpu.VMEM)] * 13,
        out_specs=pl.BlockSpec(memory_space=pltpu.VMEM),
        compiler_params=pltpu.CompilerParams(vmem_limit_bytes=24 * 1024 * 1024),
    )(
        offset, low_state, prompt_state, high_state, low_conv, conv_state, high_conv,
        mixed_input, output_gate, strength, retain, head_gain.reshape(1, -1), conv_weight,
    )
    carried = residual.reshape(rows, width).astype(jnp.float32) + jnp.dot(
        gated, out_weight, preferred_element_type=jnp.float32
    )
    normed = (
        carried
        * lax.rsqrt(jnp.mean(carried * carried, axis=-1, keepdims=True) + epsilon)
        * post_gain
    ).astype(jnp.bfloat16)
    experts = router.shape[1]
    logits = jnp.dot(normed, router, preferred_element_type=jnp.float32)
    chosen = jnp.any(
        route_ids.reshape(rows, -1, 1) == jnp.arange(experts, dtype=jnp.int32), axis=1
    )
    weights = jnp.where(chosen, jax.nn.sigmoid(logits), 0.0)
    weights = weights / jnp.sum(weights, axis=1, keepdims=True)
    high, low = halves(weights)
    extra = -(-2 * experts // 128) * 128
    tail = jnp.concatenate(
        [high, low, jnp.zeros((rows, extra - 2 * experts), jnp.float32)], axis=1
    ).astype(jnp.bfloat16)
    sending = jnp.concatenate([normed, tail], axis=1).reshape(steps, slots, width + extra)
    gathered = gathered_rows(sending, count).reshape(steps * count * slots, width + extra)
    tokens = gathered[:, :width]
    column = jnp.arange(extra, dtype=jnp.int32)
    mine = (column == me) | (column == me + experts)
    weight = jnp.sum(
        jnp.where(mine, gathered[:, width:].astype(jnp.float32), 0.0), axis=1, keepdims=True
    )
    hidden = jax.nn.silu(jnp.dot(tokens, expert_gate[0], preferred_element_type=jnp.float32))
    hidden = hidden * jnp.dot(tokens, expert_up[0], preferred_element_type=jnp.float32)
    result = jnp.dot(
        hidden.astype(jnp.bfloat16), expert_down[0], preferred_element_type=jnp.float32
    )
    result = (result * weight).astype(jnp.bfloat16)
    result = result.reshape(steps, count // 8, 2, 2, 2, slots, width)
    mixture = scattered_sum(result, count).reshape(rows, width)
    layer_out = (carried + mixture).astype(jnp.bfloat16)
    return layer_out.reshape(steps, slots, width)


def solution(mesh):
    split = P(None, ("parts", "dev"), None)
    in_specs = (
        P(("parts", "dev"), None, None, None),
        P(("parts", "dev"), None, None),
        P(("parts", "dev")),
        split, split, split, split, split,
        P(), P(), P(), P(), P(), P(), P(),
        P("dev", None, None),
        P("dev", None, None),
        P("dev", None, None),
        split,
    )
    return jax.shard_map(body, mesh=mesh, in_specs=in_specs, out_specs=split, check_vma=False)
```

```python
import functools
import math

import jax
import jax.numpy as jnp
from jax import lax
from jax.experimental import pallas as pl
from jax.experimental.pallas import tpu as pltpu
from jax.sharding import PartitionSpec as P

epsilon = 1e-06


def halves(x):
    high = lax.reduce_precision(x, 8, 7)
    return high, x - high


def delta_kernel(
    offset_ref, low_state, own_state, high_state, low_conv, own_conv, high_conv,
    mixed_ref, gate_ref, strength_ref, retain_ref, gain_ref, weight_ref, out_ref,
):
    steps, slots, _ = mixed_ref.shape
    heads, key_size, value_size = own_state.shape[1:]
    taps, channels = weight_ref.shape
    key_heads = (channels - heads * value_size) // (2 * key_size)
    share = heads // key_heads
    key_width = key_heads * key_size
    offset = offset_ref[...]
    is_low, is_high = offset == 0, offset == 2
    all_low = jnp.concatenate([is_low] * (4 * steps), axis=0)
    all_high = jnp.concatenate([is_high] * (4 * steps), axis=0)
    gain = gain_ref[...]

    def convolved(start, width):
        columns = slice(start, start + width)
        rows = []
        for j in range(taps - 1):
            own, low, high = (
                r[0, j : j + 1, columns].astype(jnp.float32) for r in (own_conv, low_conv, high_conv)
            )
            rows.append(jnp.where(is_low, low, jnp.where(is_high, high, own)))
        for t in range(steps):
            rows.append(mixed_ref[t, :, columns].astype(jnp.float32))
        results = []
        for t in range(steps):
            total = rows[t] * weight_ref[0:1, columns]
            for j in range(1, taps):
                total = total + rows[t + j] * weight_ref[j : j + 1, columns]
            results.append(total * jax.nn.sigmoid(total))
        return results

    def summed(x):
        return jnp.sum(x, axis=-1, keepdims=True)

    for group in range(key_heads):
        query = [
            x * (lax.rsqrt(summed(x * x) + epsilon) * (1.0 / math.sqrt(key_size)))
            for x in convolved(group * key_size, key_size)
        ]
        key = [
            x * lax.rsqrt(summed(x * x) + epsilon)
            for x in convolved(key_width + group * key_size, key_size)
        ]
        parts = []
        for x in query + key:
            high = x.astype(jnp.bfloat16)
            parts += [high, (x - high.astype(jnp.float32)).astype(jnp.bfloat16)]
        stacked = jnp.concatenate(parts, axis=0)
        query_key = [[summed(query[t] * key[j]) for j in range(t + 1)] for t in range(steps)]
        key_key = [[summed(key[t] * key[j]) for j in range(t)] for t in range(steps)]
        for head in range(group * share, (group + 1) * share):
            low, own, high = (
                jnp.dot(stacked, r[0, head], preferred_element_type=jnp.float32)
                for r in (low_state, own_state, high_state)
            )
            product = jnp.where(all_low, low, jnp.where(all_high, high, own))
            read = [
                product[2 * i * slots : (2 * i + 1) * slots]
                + product[(2 * i + 1) * slots : (2 * i + 2) * slots]
                for i in range(2 * steps)
            ]
            value = convolved(2 * key_width + head * value_size, value_size)
            columns = slice(head * value_size, (head + 1) * value_size)
            updates = []
            for t in range(steps):
                recalled, readout = read[steps + t], read[t]
                for j in range(t + 1):
                    retain = retain_ref[j, :, head : head + 1]
                    recalled, readout = recalled * retain, readout * retain
                    if j < t:
                        recalled = recalled + key_key[t][j] * updates[j]
                        readout = readout + query_key[t][j] * updates[j]
                update = strength_ref[t, :, head : head + 1] * (value[t] - recalled)
                updates.append(update)
                readout = readout + query_key[t][t] * update
                readout = (
                    readout
                    * lax.rsqrt(summed(readout * readout) * (1.0 / value_size) + epsilon)
                    * gain
                )
                opened = gate_ref[t, :, columns].astype(jnp.float32)
                readout = readout * (opened * jax.nn.sigmoid(opened))
                out_ref[t * slots : (t + 1) * slots, columns] = readout.astype(out_ref.dtype)


GATHER_ORDERS = (("z", "x", "y"), ("z", "y", "x"), ("y", "z", "x"))


class Place:
    def __init__(self, count):
        self.depth = count // 8
        self.me = lax.axis_index("dev")
        self.core = self.me % 2
        self.own = {"x": (self.me // 2) % 2, "y": (self.me // 4) % 2, "z": self.me // 8}
        self.sibling = self.me + 1 - 2 * self.core

    def partners(self, axis):
        if axis == "x":
            return [(self.me + 2 - 4 * self.own["x"], 1 - self.own["x"], 1 - self.own["x"])]
        if axis == "y":
            return [(self.me + 4 - 8 * self.own["y"], 1 - self.own["y"], 1 - self.own["y"])]
        found = []
        for k in range(1, self.depth):
            target = (self.own["z"] + k) % self.depth
            source = (self.own["z"] + self.depth - k) % self.depth
            found.append((target * 8 + self.me % 8, target, source))
        return found

    def meet(self):
        barrier = pltpu.get_barrier_semaphore()
        others = [self.sibling] + [p[0] for a in ("x", "y", "z") for p in self.partners(a)]
        for other in others:
            pl.semaphore_signal(
                barrier, inc=1, device_id={"dev": other}, device_id_type=pl.DeviceIdType.MESH
            )
        pl.semaphore_wait(barrier, len(others))


LANES = {"x": 0, "y": 1, "core": 2, "z": 3}


def remote(source, target, send, receive, device):
    return pltpu.make_async_remote_copy(
        src_ref=source, dst_ref=target, send_sem=send, recv_sem=receive,
        device_id={"dev": device}, device_id_type=pl.DeviceIdType.MESH,
    )


def routed_kernel(
    count, in_ref, gate_ref, up_ref, down_ref, mixture_ref, out_ref, result, fetched, total,
    from_core, from_x, from_y, from_z, local_sem, send_sem, recv_sem, back_send, back_recv,
):
    steps = in_ref.shape[0]
    place = Place(count)
    own = place.own
    local = []
    for t in range(steps):
        copy = pltpu.make_async_copy(
            in_ref.at[t], out_ref.at[t, own["z"], own["y"], own["x"], place.core], local_sem.at[t]
        )
        copy.start()
        local.append(copy)
    place.meet()
    sent = []
    arriving = [[] for _ in range(steps)]
    for stage in range(3):
        for t in range(steps):
            order = GATHER_ORDERS[t % 3]
            if stage == 0:
                local[t].wait()
            for copy in arriving[t]:
                copy.wait_recv()
            arriving[t] = []
            axis = order[stage]
            done = order[:stage]

            def region(position):
                at = [slice(None) if a in done else own[a] for a in ("z", "y", "x")]
                at[("z", "y", "x").index(axis)] = position
                return out_ref.at[t, at[0], at[1], at[2], place.core]

            for k, (device, _, source) in enumerate(place.partners(axis)):
                lane = LANES[axis] + k
                copy = remote(
                    region(own[axis]), region(own[axis]), send_sem.at[t, lane],
                    recv_sem.at[t, lane], device,
                )
                copy.start()
                sent.append(copy)
                arriving[t].append(
                    remote(
                        region(source), region(source), send_sem.at[t, lane],
                        recv_sem.at[t, lane], device,
                    )
                )

    width = down_ref.shape[1]
    slots, full = in_ref.shape[1:]
    batch = 16 * slots
    experts = count

    def compute(t):
        copy = pltpu.make_async_copy(out_ref.at[t], fetched, local_sem.at[steps])
        copy.start()
        copy.wait()

        def part(i, carry):
            span = pl.ds(2 * i, 2)
            rows = fetched[span].reshape(batch, full)
            tokens, tail = rows[:, :width], rows[:, width:].astype(jnp.float32)
            column = lax.broadcasted_iota(jnp.int32, tail.shape, 1)
            mine = (column == place.me) | (column == place.me + experts)
            weight = jnp.sum(jnp.where(mine, tail, 0.0), axis=1, keepdims=True)
            hidden = jnp.dot(tokens, gate_ref[...], preferred_element_type=jnp.float32)
            hidden = hidden * jax.nn.sigmoid(hidden)
            hidden = hidden * jnp.dot(tokens, up_ref[...], preferred_element_type=jnp.float32)
            value = jnp.dot(
                hidden.astype(jnp.bfloat16), down_ref[...], preferred_element_type=jnp.float32
            )
            value = (value * weight).astype(result.dtype)
            result[t, span] = value.reshape(2, 2, 2, 2, slots, width)
            return carry

        lax.fori_loop(0, place.depth // 2, part, 0)

    incoming = [[] for _ in range(steps)]
    landed = [None] * steps

    def advance(stage, t):
        order = GATHER_ORDERS[t % 3][::-1]
        for copy in incoming[t]:
            copy.wait_recv()
        incoming[t] = []
        done = order[:stage]
        at = [own[a] if a in done else slice(None) for a in ("z", "y", "x")]
        if stage == 0:
            value = result[t, :, :, :, place.core].astype(jnp.float32)
            value = value + from_core[t].astype(jnp.float32)
        else:
            value = total[t, at[0], at[1], at[2]].astype(jnp.float32)
            for ref, index in landed[t]:
                value = value + ref[index].astype(jnp.float32)
        if stage == 3:
            mixture_ref[t] = value
            return
        total[t, at[0], at[1], at[2]] = value.astype(total.dtype)
        axis = order[stage]
        landed[t] = []
        for k, (device, target, _) in enumerate(place.partners(axis)):
            spot = dict(zip(("z", "y", "x"), at))
            source = dict(spot)
            source[axis] = target
            if axis == "x":
                buffer, index = from_x, (t, spot["z"], spot["y"])
            elif axis == "y":
                buffer, index = from_y, (t, spot["z"], spot["x"])
            else:
                buffer, index = from_z, (t, k, spot["y"], spot["x"])
            lane = LANES[axis] + k
            copy = remote(
                total.at[t, source["z"], source["y"], source["x"]], buffer.at[index],
                back_send.at[t, lane], back_recv.at[t, lane], device,
            )
            copy.start()
            sent.append(copy)
            incoming[t].append(copy)
            landed[t].append((buffer, index))

    for t in range(steps):
        for copy in arriving[t]:
            copy.wait_recv()
        plane = out_ref.at[t, :, :, :, place.core]
        other = out_ref.at[t, :, :, :, 1 - place.core]
        sems = (send_sem.at[t, LANES["core"]], recv_sem.at[t, LANES["core"]], place.sibling)
        copy = remote(plane, plane, *sems)
        copy.start()
        sent.append(copy)
        remote(other, other, *sems).wait_recv()
        compute(t)
        copy = remote(
            result.at[t, :, :, :, 1 - place.core], from_core.at[t],
            back_send.at[t, LANES["core"]], back_recv.at[t, LANES["core"]], place.sibling,
        )
        copy.start()
        sent.append(copy)
        incoming[t].append(copy)
        if t > 0:
            advance(0, t - 1)
    advance(0, steps - 1)
    for stage in range(1, 4):
        for t in range(steps):
            advance(stage, t)
    for copy in sent:
        copy.wait_send()


def routed_sum(rows, gate, up, down, count):
    steps, slots, full = rows.shape
    width = down.shape[1]
    depth = count // 8
    sems = pltpu.SemaphoreType.DMA((steps, 2 + depth))
    whole = (depth, 2, 2, 2, slots)
    kind = rows.dtype
    vmem = pl.BlockSpec(memory_space=pltpu.VMEM)
    hbm = pl.BlockSpec(memory_space=pl.ANY)
    return pl.pallas_call(
        functools.partial(routed_kernel, count),
        out_shape=(
            jax.ShapeDtypeStruct((steps, slots, width), jnp.float32),
            jax.ShapeDtypeStruct((steps,) + whole + (full,), kind),
        ),
        in_specs=[hbm, vmem, vmem, vmem],
        out_specs=(vmem, hbm),
        scratch_shapes=[
            pltpu.VMEM((steps,) + whole + (width,), kind),
            pltpu.VMEM(whole + (full,), kind),
            pltpu.VMEM((steps, depth, 2, 2, slots, width), kind),
            pltpu.VMEM((steps, depth, 2, 2, slots, width), kind),
            pltpu.VMEM((steps, depth, 2, slots, width), kind),
            pltpu.VMEM((steps, depth, 2, slots, width), kind),
            pltpu.VMEM((steps, depth - 1, 2, 2, slots, width), kind),
            pltpu.SemaphoreType.DMA((steps + 1,)),
            sems, sems, sems, sems,
        ],
        compiler_params=pltpu.CompilerParams(
            collective_id=0, has_side_effects=True, vmem_limit_bytes=58 * 1024 * 1024
        ),
    )(rows, gate, up, down)[0]


def body(
    prompt_state, conv_state, slot_prompt, mixed_input, output_gate, residual, beta_logit,
    decay_logit, decay_base, decay_bias, head_gain, conv_weight, out_weight, post_gain, router,
    expert_gate, expert_up, expert_down, route_ids,
):
    steps, slots, width = residual.shape
    count = lax.axis_size("dev")
    me = lax.axis_index("dev")
    rows = steps * slots
    forward = [(i, i + 1) for i in range(count - 1)]
    backward = [(i + 1, i) for i in range(count - 1)]
    low_conv = lax.ppermute(conv_state, "dev", forward)
    high_conv = lax.ppermute(conv_state, "dev", backward)
    low_state = lax.ppermute(prompt_state, "dev", forward)
    high_state = lax.ppermute(prompt_state, "dev", backward)
    offset = (slot_prompt - (me - 1)).reshape(slots, 1)
    strength = jax.nn.sigmoid(beta_logit)
    retain = jnp.exp(-jnp.exp(decay_base) * jax.nn.softplus(decay_logit + decay_bias))
    heads, value_size = prompt_state.shape[1], prompt_state.shape[3]
    gated = pl.pallas_call(
        delta_kernel,
        out_shape=jax.ShapeDtypeStruct((rows, heads * value_size), jnp.bfloat16),
        in_specs=[pl.BlockSpec(memory_space=pltpu.VMEM)] * 13,
        out_specs=pl.BlockSpec(memory_space=pltpu.VMEM),
        compiler_params=pltpu.CompilerParams(vmem_limit_bytes=24 * 1024 * 1024),
    )(
        offset, low_state, prompt_state, high_state, low_conv, conv_state, high_conv,
        mixed_input, output_gate, strength, retain, head_gain.reshape(1, -1), conv_weight,
    )
    carried = residual.reshape(rows, width).astype(jnp.float32) + jnp.dot(
        gated, out_weight, preferred_element_type=jnp.float32
    )
    normed = (
        carried
        * lax.rsqrt(jnp.mean(carried * carried, axis=-1, keepdims=True) + epsilon)
        * post_gain
    ).astype(jnp.bfloat16)
    experts = router.shape[1]
    logits = jnp.dot(normed, router, preferred_element_type=jnp.float32)
    chosen = jnp.any(
        route_ids.reshape(rows, -1, 1) == jnp.arange(experts, dtype=jnp.int32), axis=1
    )
    weights = jnp.where(chosen, jax.nn.sigmoid(logits), 0.0)
    weights = weights / jnp.sum(weights, axis=1, keepdims=True)
    high, low = halves(weights)
    extra = -(-2 * experts // 128) * 128
    tail = jnp.concatenate(
        [high, low, jnp.zeros((rows, extra - 2 * experts), jnp.float32)], axis=1
    ).astype(jnp.bfloat16)
    sending = jnp.concatenate([normed, tail], axis=1).reshape(steps, slots, width + extra)
    mixture = routed_sum(sending, expert_gate[0], expert_up[0], expert_down[0], count)
    mixture = mixture.reshape(rows, width)
    layer_out = (carried + mixture).astype(jnp.bfloat16)
    return layer_out.reshape(steps, slots, width)


def solution(mesh):
    split = P(None, ("parts", "dev"), None)
    in_specs = (
        P(("parts", "dev"), None, None, None),
        P(("parts", "dev"), None, None),
        P(("parts", "dev")),
        split, split, split, split, split,
        P(), P(), P(), P(), P(), P(), P(),
        P("dev", None, None),
        P("dev", None, None),
        P("dev", None, None),
        split,
    )
    return jax.shard_map(body, mesh=mesh, in_specs=in_specs, out_specs=split, check_vma=False)
```

```python
import functools
import math

import jax
import jax.numpy as jnp
from jax import lax
from jax.experimental import pallas as pl
from jax.experimental.pallas import tpu as pltpu
from jax.sharding import PartitionSpec as P

epsilon = 1e-06


def halves(x):
    high = lax.reduce_precision(x, 8, 7)
    return high, x - high


def delta_kernel(
    offset_ref, low_state, own_state, high_state, low_conv, own_conv, high_conv,
    mixed_ref, gate_ref, strength_ref, retain_ref, gain_ref, weight_ref, out_ref,
):
    steps, slots, _ = mixed_ref.shape
    heads, key_size, value_size = own_state.shape[1:]
    taps, channels = weight_ref.shape
    key_heads = (channels - heads * value_size) // (2 * key_size)
    share = heads // key_heads
    key_width = key_heads * key_size
    offset = offset_ref[...]
    is_low, is_high = offset == 0, offset == 2
    all_low = jnp.concatenate([is_low] * (4 * steps), axis=0)
    all_high = jnp.concatenate([is_high] * (4 * steps), axis=0)
    gain = gain_ref[...]

    def convolved(start, width):
        columns = slice(start, start + width)
        rows = []
        for j in range(taps - 1):
            own, low, high = (
                r[0, j : j + 1, columns].astype(jnp.float32) for r in (own_conv, low_conv, high_conv)
            )
            rows.append(jnp.where(is_low, low, jnp.where(is_high, high, own)))
        for t in range(steps):
            rows.append(mixed_ref[t, :, columns].astype(jnp.float32))
        results = []
        for t in range(steps):
            total = rows[t] * weight_ref[0:1, columns]
            for j in range(1, taps):
                total = total + rows[t + j] * weight_ref[j : j + 1, columns]
            results.append(total * jax.nn.sigmoid(total))
        return results

    def summed(x):
        return jnp.sum(x, axis=-1, keepdims=True)

    for group in range(key_heads):
        query = [
            x * (lax.rsqrt(summed(x * x) + epsilon) * (1.0 / math.sqrt(key_size)))
            for x in convolved(group * key_size, key_size)
        ]
        key = [
            x * lax.rsqrt(summed(x * x) + epsilon)
            for x in convolved(key_width + group * key_size, key_size)
        ]
        parts = []
        for x in query + key:
            high = x.astype(jnp.bfloat16)
            parts += [high, (x - high.astype(jnp.float32)).astype(jnp.bfloat16)]
        stacked = jnp.concatenate(parts, axis=0)
        query_key = [[summed(query[t] * key[j]) for j in range(t + 1)] for t in range(steps)]
        key_key = [[summed(key[t] * key[j]) for j in range(t)] for t in range(steps)]
        for head in range(group * share, (group + 1) * share):
            low, own, high = (
                jnp.dot(stacked, r[0, head], preferred_element_type=jnp.float32)
                for r in (low_state, own_state, high_state)
            )
            product = jnp.where(all_low, low, jnp.where(all_high, high, own))
            read = [
                product[2 * i * slots : (2 * i + 1) * slots]
                + product[(2 * i + 1) * slots : (2 * i + 2) * slots]
                for i in range(2 * steps)
            ]
            value = convolved(2 * key_width + head * value_size, value_size)
            columns = slice(head * value_size, (head + 1) * value_size)
            updates = []
            for t in range(steps):
                recalled, readout = read[steps + t], read[t]
                for j in range(t + 1):
                    retain = retain_ref[j, :, head : head + 1]
                    recalled, readout = recalled * retain, readout * retain
                    if j < t:
                        recalled = recalled + key_key[t][j] * updates[j]
                        readout = readout + query_key[t][j] * updates[j]
                update = strength_ref[t, :, head : head + 1] * (value[t] - recalled)
                updates.append(update)
                readout = readout + query_key[t][t] * update
                readout = (
                    readout
                    * lax.rsqrt(summed(readout * readout) * (1.0 / value_size) + epsilon)
                    * gain
                )
                opened = gate_ref[t, :, columns].astype(jnp.float32)
                readout = readout * (opened * jax.nn.sigmoid(opened))
                out_ref[t * slots : (t + 1) * slots, columns] = readout.astype(out_ref.dtype)


GATHER_ORDERS = (("z", "x", "y"), ("z", "y", "x"), ("y", "z", "x"))


class Place:
    def __init__(self, count):
        self.depth = count // 8
        self.me = lax.axis_index("dev")
        self.core = self.me % 2
        self.own = {"x": (self.me // 2) % 2, "y": (self.me // 4) % 2, "z": self.me // 8}
        self.sibling = self.me + 1 - 2 * self.core

    def partners(self, axis):
        if axis == "x":
            return [(self.me + 2 - 4 * self.own["x"], 1 - self.own["x"], 1 - self.own["x"])]
        if axis == "y":
            return [(self.me + 4 - 8 * self.own["y"], 1 - self.own["y"], 1 - self.own["y"])]
        found = []
        for k in range(1, self.depth):
            target = (self.own["z"] + k) % self.depth
            source = (self.own["z"] + self.depth - k) % self.depth
            found.append((target * 8 + self.me % 8, target, source))
        return found

    def meet(self):
        barrier = pltpu.get_barrier_semaphore()
        others = [self.sibling] + [p[0] for a in ("x", "y", "z") for p in self.partners(a)]
        for other in others:
            pl.semaphore_signal(
                barrier, inc=1, device_id={"dev": other}, device_id_type=pl.DeviceIdType.MESH
            )
        pl.semaphore_wait(barrier, len(others))


LANES = {"x": 0, "y": 1, "core": 2, "z": 3}


def remote(source, target, send, receive, device):
    return pltpu.make_async_remote_copy(
        src_ref=source, dst_ref=target, send_sem=send, recv_sem=receive,
        device_id={"dev": device}, device_id_type=pl.DeviceIdType.MESH,
    )


def neighbour_kernel(
    count, state, conv, low_state, high_state, low_conv, high_conv, send_sem, recv_sem
):
    me = lax.axis_index("dev")
    low, high = (me + count - 1) % count, (me + 1) % count
    barrier = pltpu.get_barrier_semaphore()
    for other in (low, high):
        pl.semaphore_signal(
            barrier, inc=1, device_id={"dev": other}, device_id_type=pl.DeviceIdType.MESH
        )
    pl.semaphore_wait(barrier, 2)
    moves = (
        (state, low_state, high), (state, high_state, low),
        (conv, low_conv, high), (conv, high_conv, low),
    )
    copies = [
        remote(source, target, send_sem.at[i], recv_sem.at[i], device)
        for i, (source, target, device) in enumerate(moves)
    ]
    for copy in copies:
        copy.start()
    for copy in copies:
        copy.wait()


def neighbours(state, conv, count):
    hbm = pl.BlockSpec(memory_space=pl.ANY)
    kinds = [jax.ShapeDtypeStruct(a.shape, a.dtype) for a in (state, state, conv, conv)]
    return pl.pallas_call(
        functools.partial(neighbour_kernel, count),
        out_shape=kinds,
        in_specs=[hbm] * 2,
        out_specs=[hbm] * 4,
        scratch_shapes=[pltpu.SemaphoreType.DMA((4,)), pltpu.SemaphoreType.DMA((4,))],
        compiler_params=pltpu.CompilerParams(collective_id=1, has_side_effects=True),
    )(state, conv)


def routed_kernel(
    count, in_ref, gate_ref, up_ref, down_ref, mixture_ref, out_ref, result, fetched, total,
    from_core, from_x, from_y, from_z, local_sem, send_sem, recv_sem, back_send, back_recv,
):
    steps = in_ref.shape[0]
    place = Place(count)
    own = place.own
    local = []
    for t in range(steps):
        copy = pltpu.make_async_copy(
            in_ref.at[t], out_ref.at[t, own["z"], own["y"], own["x"], place.core], local_sem.at[t]
        )
        copy.start()
        local.append(copy)
    place.meet()
    sent = []
    arriving = [[] for _ in range(steps)]
    for stage in range(3):
        for t in range(steps):
            order = GATHER_ORDERS[t % 3]
            if stage == 0:
                local[t].wait()
            for copy in arriving[t]:
                copy.wait_recv()
            arriving[t] = []
            axis = order[stage]
            done = order[:stage]

            def region(position):
                at = [slice(None) if a in done else own[a] for a in ("z", "y", "x")]
                at[("z", "y", "x").index(axis)] = position
                return out_ref.at[t, at[0], at[1], at[2], place.core]

            for k, (device, _, source) in enumerate(place.partners(axis)):
                lane = LANES[axis] + k
                copy = remote(
                    region(own[axis]), region(own[axis]), send_sem.at[t, lane],
                    recv_sem.at[t, lane], device,
                )
                copy.start()
                sent.append(copy)
                arriving[t].append(
                    remote(
                        region(source), region(source), send_sem.at[t, lane],
                        recv_sem.at[t, lane], device,
                    )
                )

    width = down_ref.shape[1]
    slots, full = in_ref.shape[1:]
    batch = 16 * slots
    experts = count

    def compute(t):
        copy = pltpu.make_async_copy(out_ref.at[t], fetched, local_sem.at[steps])
        copy.start()
        copy.wait()

        def part(i, carry):
            span = pl.ds(2 * i, 2)
            rows = fetched[span].reshape(batch, full)
            tokens, tail = rows[:, :width], rows[:, width:].astype(jnp.float32)
            column = lax.broadcasted_iota(jnp.int32, tail.shape, 1)
            mine = (column == place.me) | (column == place.me + experts)
            weight = jnp.sum(jnp.where(mine, tail, 0.0), axis=1, keepdims=True)
            hidden = jnp.dot(tokens, gate_ref[...], preferred_element_type=jnp.float32)
            hidden = hidden * jax.nn.sigmoid(hidden)
            hidden = hidden * jnp.dot(tokens, up_ref[...], preferred_element_type=jnp.float32)
            value = jnp.dot(
                hidden.astype(jnp.bfloat16), down_ref[...], preferred_element_type=jnp.float32
            )
            value = (value * weight).astype(result.dtype)
            result[t, span] = value.reshape(2, 2, 2, 2, slots, width)
            return carry

        lax.fori_loop(0, place.depth // 2, part, 0)

    incoming = [[] for _ in range(steps)]
    landed = [None] * steps

    def advance(stage, t):
        order = GATHER_ORDERS[t % 3][::-1]
        for copy in incoming[t]:
            copy.wait_recv()
        incoming[t] = []
        done = order[:stage]
        at = [own[a] if a in done else slice(None) for a in ("z", "y", "x")]
        if stage == 0:
            value = result[t, :, :, :, place.core].astype(jnp.float32)
            value = value + from_core[t].astype(jnp.float32)
        else:
            value = total[t, at[0], at[1], at[2]].astype(jnp.float32)
            for ref, index in landed[t]:
                value = value + ref[index].astype(jnp.float32)
        if stage == 3:
            mixture_ref[t] = value
            return
        total[t, at[0], at[1], at[2]] = value.astype(total.dtype)
        axis = order[stage]
        landed[t] = []
        for k, (device, target, _) in enumerate(place.partners(axis)):
            spot = dict(zip(("z", "y", "x"), at))
            source = dict(spot)
            source[axis] = target
            if axis == "x":
                buffer, index = from_x, (t, spot["z"], spot["y"])
            elif axis == "y":
                buffer, index = from_y, (t, spot["z"], spot["x"])
            else:
                buffer, index = from_z, (t, k, spot["y"], spot["x"])
            lane = LANES[axis] + k
            copy = remote(
                total.at[t, source["z"], source["y"], source["x"]], buffer.at[index],
                back_send.at[t, lane], back_recv.at[t, lane], device,
            )
            copy.start()
            sent.append(copy)
            incoming[t].append(copy)
            landed[t].append((buffer, index))

    for t in range(steps):
        for copy in arriving[t]:
            copy.wait_recv()
        plane = out_ref.at[t, :, :, :, place.core]
        other = out_ref.at[t, :, :, :, 1 - place.core]
        sems = (send_sem.at[t, LANES["core"]], recv_sem.at[t, LANES["core"]], place.sibling)
        copy = remote(plane, plane, *sems)
        copy.start()
        sent.append(copy)
        remote(other, other, *sems).wait_recv()
        compute(t)
        copy = remote(
            result.at[t, :, :, :, 1 - place.core], from_core.at[t],
            back_send.at[t, LANES["core"]], back_recv.at[t, LANES["core"]], place.sibling,
        )
        copy.start()
        sent.append(copy)
        incoming[t].append(copy)
        if t > 0:
            advance(0, t - 1)
    advance(0, steps - 1)
    for stage in range(1, 4):
        for t in range(steps):
            advance(stage, t)
    for copy in sent:
        copy.wait_send()


def routed_sum(rows, gate, up, down, count):
    steps, slots, full = rows.shape
    width = down.shape[1]
    depth = count // 8
    sems = pltpu.SemaphoreType.DMA((steps, 2 + depth))
    whole = (depth, 2, 2, 2, slots)
    kind = rows.dtype
    vmem = pl.BlockSpec(memory_space=pltpu.VMEM)
    hbm = pl.BlockSpec(memory_space=pl.ANY)
    return pl.pallas_call(
        functools.partial(routed_kernel, count),
        out_shape=(
            jax.ShapeDtypeStruct((steps, slots, width), jnp.float32),
            jax.ShapeDtypeStruct((steps,) + whole + (full,), kind),
        ),
        in_specs=[hbm, vmem, vmem, vmem],
        out_specs=(vmem, hbm),
        scratch_shapes=[
            pltpu.VMEM((steps,) + whole + (width,), kind),
            pltpu.VMEM(whole + (full,), kind),
            pltpu.VMEM((steps, depth, 2, 2, slots, width), kind),
            pltpu.VMEM((steps, depth, 2, 2, slots, width), kind),
            pltpu.VMEM((steps, depth, 2, slots, width), kind),
            pltpu.VMEM((steps, depth, 2, slots, width), kind),
            pltpu.VMEM((steps, depth - 1, 2, 2, slots, width), kind),
            pltpu.SemaphoreType.DMA((steps + 1,)),
            sems, sems, sems, sems,
        ],
        compiler_params=pltpu.CompilerParams(
            collective_id=0, has_side_effects=True, vmem_limit_bytes=58 * 1024 * 1024
        ),
    )(rows, gate, up, down)[0]


def body(
    prompt_state, conv_state, slot_prompt, mixed_input, output_gate, residual, beta_logit,
    decay_logit, decay_base, decay_bias, head_gain, conv_weight, out_weight, post_gain, router,
    expert_gate, expert_up, expert_down, route_ids,
):
    steps, slots, width = residual.shape
    count = lax.axis_size("dev")
    me = lax.axis_index("dev")
    rows = steps * slots
    conv_lines = conv_state.reshape(-1, 128)
    low_state, high_state, low_conv, high_conv = neighbours(prompt_state, conv_lines, count)
    low_conv, high_conv = low_conv.reshape(conv_state.shape), high_conv.reshape(conv_state.shape)
    offset = (slot_prompt - (me - 1)).reshape(slots, 1)
    strength = jax.nn.sigmoid(beta_logit)
    retain = jnp.exp(-jnp.exp(decay_base) * jax.nn.softplus(decay_logit + decay_bias))
    heads, value_size = prompt_state.shape[1], prompt_state.shape[3]
    gated = pl.pallas_call(
        delta_kernel,
        out_shape=jax.ShapeDtypeStruct((rows, heads * value_size), jnp.bfloat16),
        in_specs=[pl.BlockSpec(memory_space=pltpu.VMEM)] * 13,
        out_specs=pl.BlockSpec(memory_space=pltpu.VMEM),
        compiler_params=pltpu.CompilerParams(vmem_limit_bytes=24 * 1024 * 1024),
    )(
        offset, low_state, prompt_state, high_state, low_conv, conv_state, high_conv,
        mixed_input, output_gate, strength, retain, head_gain.reshape(1, -1), conv_weight,
    )
    carried = residual.reshape(rows, width).astype(jnp.float32) + jnp.dot(
        gated, out_weight, preferred_element_type=jnp.float32
    )
    normed = (
        carried
        * lax.rsqrt(jnp.mean(carried * carried, axis=-1, keepdims=True) + epsilon)
        * post_gain
    ).astype(jnp.bfloat16)
    experts = router.shape[1]
    logits = jnp.dot(normed, router, preferred_element_type=jnp.float32)
    chosen = jnp.any(
        route_ids.reshape(rows, -1, 1) == jnp.arange(experts, dtype=jnp.int32), axis=1
    )
    weights = jnp.where(chosen, jax.nn.sigmoid(logits), 0.0)
    weights = weights / jnp.sum(weights, axis=1, keepdims=True)
    high, low = halves(weights)
    extra = -(-2 * experts // 128) * 128
    tail = jnp.concatenate(
        [high, low, jnp.zeros((rows, extra - 2 * experts), jnp.float32)], axis=1
    ).astype(jnp.bfloat16)
    sending = jnp.concatenate([normed, tail], axis=1).reshape(steps, slots, width + extra)
    mixture = routed_sum(sending, expert_gate[0], expert_up[0], expert_down[0], count)
    mixture = mixture.reshape(rows, width)
    layer_out = (carried + mixture).astype(jnp.bfloat16)
    return layer_out.reshape(steps, slots, width)


def solution(mesh):
    split = P(None, ("parts", "dev"), None)
    in_specs = (
        P(("parts", "dev"), None, None, None),
        P(("parts", "dev"), None, None),
        P(("parts", "dev")),
        split, split, split, split, split,
        P(), P(), P(), P(), P(), P(), P(),
        P("dev", None, None),
        P("dev", None, None),
        P("dev", None, None),
        split,
    )
    return jax.shard_map(body, mesh=mesh, in_specs=in_specs, out_specs=split, check_vma=False)
```
